128 devices in a mesh: fsdp: 128 (over z, y, x, core).
Axes of the slice: x: 4, y: 4, z: 4, core: 2. Of those that a mesh axis runs over, the one named last changes fastest.
Arguments:
- images: bfloat16 [384, 197, 768], P('fsdp'), may hold values from -6 to 6
- counts: int32 [128], P('fsdp'), may hold values from 2 to 3, as said below
- ln1_gain: bfloat16 [768], P('fsdp'), may hold values from 0.5 to 1.5
- ln1_bias: bfloat16 [768], P('fsdp'), may hold values from -1.1953125 to 1.1953125
- qkv_weight: bfloat16 [768, 2304], P('fsdp'), may hold values from -0.21875 to 0.21875
- qkv_bias: bfloat16 [1536], P('fsdp'), may hold values from -1.1953125 to 1.1953125
- out_weight: bfloat16 [768, 768], P('fsdp'), may hold values from -0.625 to 0.625
- out_bias: bfloat16 [768], P('fsdp'), may hold values from -1.1953125 to 1.1953125
- ln2_gain: bfloat16 [768], P('fsdp'), may hold values from 0.5 to 1.5
- ln2_bias: bfloat16 [768], P('fsdp'), may hold values from -1.1953125 to 1.1953125
- fc1_weight: bfloat16 [768, 3072], P('fsdp'), may hold values from -0.21875 to 0.21875
- fc1_bias: bfloat16 [3072], P('fsdp'), may hold values from -1.1953125 to 1.1953125
- fc2_weight: bfloat16 [3072, 768], P('fsdp'), may hold values from -0.109375 to 0.109375
- fc2_bias: bfloat16 [768], P('fsdp'), may hold values from -1.1953125 to 1.1953125
- d_out: bfloat16 [384, 197, 768], P('fsdp'), may hold values from -6 to 6
Outputs:
- out_images: bfloat16 [384, 197, 768], P('fsdp')
- d_images: bfloat16 [384, 197, 768], P('fsdp')
- d_ln1_gain: float32 [768], P('fsdp')
- d_ln1_bias: float32 [768], P('fsdp')
- d_qkv_weight: float32 [768, 2304], P('fsdp')
- d_qkv_bias: float32 [1536], P('fsdp')
- d_out_weight: float32 [768, 768], P('fsdp')
- d_out_bias: float32 [768], P('fsdp')
- d_ln2_gain: float32 [768], P('fsdp')
- d_ln2_bias: float32 [768], P('fsdp')
- d_fc1_weight: float32 [768, 3072], P('fsdp')
- d_fc1_bias: float32 [3072], P('fsdp')
- d_fc2_weight: float32 [3072, 768], P('fsdp')
- d_fc2_bias: float32 [768], P('fsdp')
The draws below stay inside these ranges and needn't reach their ends.
Inputs may be any that keep to these rules, and one draw needn't show every extreme that they name: `counts`: each device holds 2 or 3 images in its first slots; some device holds each of the two numbers.
All inputs are finite; a program needn't handle non-finite values.
Results may differ from the reference program's by a relative error of at most 0.019.
Values may be sent and summed in bfloat16 or wider, within the bound.
No kernel may reach another device: no remote copies, remote signals or barrier semaphores. Data moves between devices by JAX's collectives and lax.ppermute only.
A program may use at most 192 MiB of HBM per device.

```python
import math
import jax
import jax.numpy as jnp
from jax import lax

D = 768
H = 12
HD = 64
FF = 3072
SEQ = 197
IMG_DEV = 3
IMAGES = 384
N_FSDP = 128


def draw_counts(key, part):
    key_first, key_order = jax.random.split(key)
    drawn_counts = jax.random.randint(key_first, (N_FSDP,), IMG_DEV - 1, IMG_DEV + 1)
    ordering = jax.random.permutation(key_order, N_FSDP)
    drawn_counts = drawn_counts.at[ordering[0]].set(IMG_DEV)
    drawn_counts = drawn_counts.at[ordering[1]].set(IMG_DEV - 1)
    return drawn_counts.astype(jnp.int32)


def shard_levels(own_key, shape, cuts, low, high):
    factor_of, own = 1.0, jax.random.fold_in(own_key, 6)
    for axis_at, shards_of in cuts:
        draws = jnp.exp(jax.random.uniform(jax.random.fold_in(own, axis_at), (shards_of,), jnp.float32, low / len(cuts), high / len(cuts)))
        factor_of = factor_of * jnp.repeat(draws, shape[axis_at] // shards_of).reshape([-1 if axis == axis_at else 1 for axis in range(len(shape))])
    return factor_of


def gaussian(own_key, extent, deviation, limit, cuts=(), kind=jnp.bfloat16):
    values = jax.random.normal(own_key, extent, jnp.float32) * deviation
    if len(cuts) > 0:
        values = shard_levels(own_key, extent, cuts, -0.22, 0.18) * values
    return jnp.clip(values, min=-limit, max=limit).astype(kind)


def setup_inputs(seed: int = 0) -> dict:
    splits = jax.random.split(jax.random.key(seed), 16)
    return {
        "images": gaussian(splits[0], (IMAGES, SEQ, D), 1.0, 6.0, ((0, 128),)),
        "counts": draw_counts(jax.random.fold_in(splits[15], 71), 0),
        "ln1_gain": jnp.clip(1.0 + 0.1 * jax.random.normal(splits[2], (D,), jnp.float32), 0.5, 1.5).astype(jnp.bfloat16),
        "ln1_bias": gaussian(splits[3], (D,), 0.2, 1.1953125, ((0, 128),)),
        "qkv_weight": gaussian(splits[4], (D, 3 * D), D ** -0.5, 0.21875, ((0, 128),)),
        "qkv_bias": gaussian(splits[5], (2 * D,), 0.2, 1.1953125, ((0, 128),)),
        "out_weight": gaussian(splits[6], (D, D), (D // 8) ** -0.5, 0.625, ((0, 128),)),
        "out_bias": gaussian(splits[7], (D,), 0.2, 1.1953125, ((0, 128),)),
        "ln2_gain": jnp.clip(1.0 + 0.1 * jax.random.normal(splits[8], (D,), jnp.float32), 0.5, 1.5).astype(jnp.bfloat16),
        "ln2_bias": gaussian(splits[9], (D,), 0.2, 1.1953125, ((0, 128),)),
        "fc1_weight": gaussian(splits[10], (D, FF), D ** -0.5, 0.21875, ((0, 128),)),
        "fc1_bias": gaussian(splits[11], (FF,), 0.2, 1.1953125, ((0, 128),)),
        "fc2_weight": gaussian(splits[12], (FF, D), FF ** -0.5, 0.109375, ((0, 128),)),
        "fc2_bias": gaussian(splits[13], (D,), 0.2, 1.1953125, ((0, 128),)),
        "d_out": gaussian(splits[14], (IMAGES, SEQ, D), 1.0, 6.0, ((0, 128),)),
    }


eps_norm = 1e-06

@jax.custom_vjp
def low(v):
    return lax.optimization_barrier(v.astype(jnp.bfloat16)).astype(jnp.float32)

@jax.custom_vjp
def low_back(v):
    return v

def low_keep(v):
    return (low(v), None)

def low_pass(kept, grad):
    return (grad,)

def back_keep(v):
    return (v, None)

def back_low(kept, grad):
    return (low(grad),)
low.defvjp(low_keep, low_pass)
low_back.defvjp(back_keep, back_low)

def normalize(values, gain_vec, offset):
    average = lax.optimization_barrier(jnp.mean(values, -1, keepdims=True))
    centered = values - average
    spread = lax.optimization_barrier(jnp.mean(centered * centered, -1, keepdims=True))
    return centered * lax.rsqrt(spread + eps_norm) * gain_vec + offset

def matmul(left, right):
    return jnp.dot(left, right, precision=lax.Precision.HIGHEST)

def image_group(inputs, params, slot_live):
    gain_one, offset_one, qkv_matrix, qkv_offset, out_matrix, out_offset, gain_two, offset_two, fc1_matrix, fc1_offset, fc2_matrix, fc2_offset = params
    slot_count = inputs.shape[0]
    tokens_flat = inputs.reshape(slot_count * SEQ, D)
    normed_one = low(normalize(tokens_flat, gain_one, offset_one))
    bias_full = jnp.concatenate([qkv_offset[:D], jnp.zeros((D,), jnp.float32), qkv_offset[D:]])
    project = low(low_back(matmul(normed_one, qkv_matrix) + bias_full))
    queries = project[:, :D].reshape(slot_count, SEQ, H, HD)
    key_heads = project[:, D:2 * D].reshape(slot_count, SEQ, H, HD)
    value_heads = project[:, 2 * D:].reshape(slot_count, SEQ, H, HD)
    score_scale = 1.0 / math.sqrt(HD)
    scores = low_back(jnp.einsum('gqhd,gkhd->ghqk', queries, key_heads, precision=lax.Precision.HIGHEST) * score_scale)
    attn_probs = jnp.exp(scores - jax.nn.logsumexp(scores, axis=-1, keepdims=True))
    mixed_heads = jnp.einsum('ghqk,gkhd->gqhd', low(attn_probs), value_heads, precision=lax.Precision.HIGHEST)
    mixed_heads = low(low_back(mixed_heads.reshape(slot_count * SEQ, D)))
    after_attn = tokens_flat + low_back(matmul(mixed_heads, out_matrix) + out_offset)
    normed_two = low(normalize(after_attn, gain_two, offset_two))
    pre_act = low_back(matmul(normed_two, fc1_matrix) + fc1_offset)
    hidden = low(jax.nn.gelu(pre_act, approximate=False))
    branch_two = low_back(matmul(hidden, fc2_matrix) + fc2_offset)
    outcome = (after_attn + branch_two).reshape(slot_count, SEQ, D)
    return outcome * slot_live[:, None, None]

def reference(images, counts, ln1_gain, ln1_bias, qkv_weight, qkv_bias, out_weight, out_bias, ln2_gain, ln2_bias, fc1_weight, fc1_bias, fc2_weight, fc2_bias, d_out):
    slot_live = (jnp.arange(IMG_DEV, dtype=jnp.int32)[None, :] < counts[:, None]).astype(jnp.float32)
    grouped = images.astype(jnp.float32).reshape(N_FSDP, IMG_DEV, SEQ, D)
    params = tuple((item.astype(jnp.float32) for item in (ln1_gain, ln1_bias, qkv_weight, qkv_bias, out_weight, out_bias, ln2_gain, ln2_bias, fc1_weight, fc1_bias, fc2_weight, fc2_bias)))
    blocked = jax.checkpoint(image_group)

    def forward(group_inputs, weights_all):

        def one_group(pair):
            return blocked(pair[0], weights_all, pair[1])
        return lax.map(one_group, (group_inputs, slot_live))
    result, pullback = jax.vjp(forward, grouped, params)
    cotangent = d_out.astype(jnp.float32).reshape(N_FSDP, IMG_DEV, SEQ, D)
    grad_inputs, grad_params = pullback(cotangent)
    out_images = result.reshape(IMAGES, SEQ, D).astype(jnp.bfloat16)
    d_images = grad_inputs.reshape(IMAGES, SEQ, D).astype(jnp.bfloat16)
    return (out_images, d_images, grad_params[0], grad_params[1], grad_params[2], grad_params[3], grad_params[4], grad_params[5], grad_params[6], grad_params[7], grad_params[8], grad_params[9], grad_params[10], grad_params[11])
```

```python
import math

import jax
import jax.numpy as jnp
import numpy as np
from jax import lax
from jax.sharding import PartitionSpec as P

H = 12
HD = 64


eps_norm = 1e-06


def normalize(values, gain_vec, offset):
    average = jnp.mean(values, -1, keepdims=True)
    centered = values - average
    spread = jnp.mean(centered * centered, -1, keepdims=True)
    return centered * lax.rsqrt(spread + eps_norm) * gain_vec + offset


def exact_gelu(values):
    return jax.nn.gelu(values, approximate=False)


def mat_product(left, right):
    return jnp.dot(left, right, preferred_element_type=jnp.float32)


def grad_weight(left, right):
    return jnp.einsum("ra,rb->ab", left, right, preferred_element_type=jnp.float32)


def grad_input(grad_low, matrix):
    return jnp.einsum("rb,ab->ra", grad_low, matrix, preferred_element_type=jnp.float32)


def column_sums(grad_low):
    return jnp.sum(grad_low, axis=0, dtype=jnp.float32)


def torus_perm(axis, offset):
    grid = np.arange(128).reshape(4, 4, 4, 2)
    dim = {"z": 0, "y": 1, "x": 2, "core": 3}[axis]
    return list(zip(grid.reshape(-1).tolist(), np.roll(grid, -offset, dim).reshape(-1).tolist()))


def coord(axis):
    stride, size = {"z": (32, 4), "y": (8, 4), "x": (2, 4), "core": (1, 2)}[axis]
    return lax.rem(lax.div(lax.axis_index("fsdp"), jnp.int32(stride)), jnp.int32(size))


PLANE_GROUPS = np.arange(128).reshape(16, 8).T.tolist()


def send(values, axis, offset):
    return lax.ppermute(values, "fsdp", torus_perm(axis, offset))


def up(values):
    return values.astype(jnp.float32)


def down(values):
    return values.astype(jnp.bfloat16)


def block(values, index, dim):
    return lax.dynamic_index_in_dim(values, index, dim, keepdims=False)


def chunks(values, axis, dim):
    own = coord(axis)
    return [block(values, lax.rem(own + k, jnp.int32(4)), dim) for k in range(4)]


def sum_ring(values, axis, dim):
    own, one, two, three = chunks(values, axis, dim)
    half = own.shape[-2] // 16 * 8
    lo = lambda v: v[..., :half, :]
    hi = lambda v: v[..., half:, :]
    fore = send(jnp.concatenate([lo(two), hi(one)], -2), axis, 1)
    back = send(jnp.concatenate([hi(two), lo(three)], -2), axis, -1)
    rest = own.shape[-2] - half
    fore_end = send(down(up(lo(one)) + up(lo(fore))), axis, 1)
    back_end = send(down(up(hi(three)) + up(back[..., :rest, :])), axis, -1)
    low = up(lo(own)) + up(back[..., rest:, :]) + up(fore_end)
    high = up(hi(own)) + up(hi(fore)) + up(back_end)
    return down(jnp.concatenate([low, high], -2))


def sum_direct(values, axis, dim):
    own, one, two, three = chunks(values, axis, dim)
    return up(own) + up(send(one, axis, 1)) + up(send(two, axis, 2)) + up(send(three, axis, -1))


def pair_grad(left, right):
    core = coord("core")
    width = right.shape[1] // 2
    other = lax.dynamic_slice_in_dim(right, (1 - core) * width, width, 1)
    mine = lax.dynamic_slice_in_dim(right, core * width, width, 1)
    arrived = send(down(grad_weight(left, other)), "core", 1)
    return down(grad_weight(left, mine) + up(arrived))


def pair_join(mine, theirs, axis):
    first = coord("core") == 0
    return jnp.concatenate([jnp.where(first, mine, theirs), jnp.where(first, theirs, mine)], axis)


def early_sums(fc2, fc1, out, small):
    packed = jnp.concatenate(
        [
            fc2.reshape(16, 192, 384),
            fc1.reshape(16, 48, 4, 384).transpose(0, 2, 1, 3).reshape(16, 192, 384),
            out.reshape(16, 48, 384),
            jnp.pad(down(small).reshape(16, 1, 384), ((0, 0), (0, 15), (0, 0))),
        ],
        axis=1,
    ).reshape(16 * 448, 384)
    part = lax.psum_scatter(
        packed, "fsdp", scatter_dimension=0, axis_index_groups=PLANE_GROUPS, tiled=True
    )
    rows = jnp.concatenate(
        [
            part[:192].reshape(4, 48, 384),
            part[192:384].reshape(4, 4, 12, 384).transpose(1, 0, 2, 3).reshape(4, 48, 384),
            part[384:432].reshape(4, 12, 384),
            jnp.pad(part[432].reshape(4, 1, 96), ((0, 0), (0, 3), (0, 288))),
        ],
        axis=1,
    )
    rows = sum_direct(rows, "x", 0)
    packed = jnp.concatenate(
        [
            rows[:48].reshape(2, 24, 384),
            rows[48:96].reshape(4, 2, 6, 384).transpose(1, 0, 2, 3).reshape(2, 24, 384),
            rows[96:108].reshape(2, 6, 384),
            jnp.pad(rows[108, :96].reshape(2, 1, 48), ((0, 0), (0, 1), (0, 336))),
        ],
        axis=1,
    )
    core = coord("core")
    mine = block(packed, core, 0)
    theirs = send(block(packed, 1 - core, 0), "core", 1)
    fc2_own = pair_join(mine[:24], theirs[:24], 1)
    fc1_rows = lambda v: v[24:48].reshape(4, 6, 384).transpose(1, 0, 2).reshape(6, 1536)
    fc1_own = pair_join(fc1_rows(mine), fc1_rows(theirs), 1)
    out_own = pair_join(mine[48:54], theirs[48:54], 1)
    small_own = mine[54, :48] + theirs[54, :48]
    return fc2_own, fc1_own, out_own, small_own


def late_sums(qkv, small):
    packed = jnp.concatenate(
        [
            qkv.reshape(16, 48, 3, 384).transpose(0, 2, 1, 3).reshape(16, 144, 384),
            jnp.pad(down(small).reshape(16, 1, 192), ((0, 0), (0, 7), (0, 192))),
        ],
        axis=1,
    ).reshape(4, 4, 152, 384)
    first = down(sum_direct(sum_ring(packed[:, :, :80], "z", 0), "y", 0))
    second = down(sum_direct(sum_ring(packed[:, :, 80:], "y", 1), "z", 0))
    part = jnp.concatenate([first, second], 0)
    rows = jnp.concatenate(
        [
            part[:144].reshape(3, 4, 12, 384).transpose(1, 0, 2, 3).reshape(4, 36, 384),
            jnp.pad(part[144, :192].reshape(4, 1, 48), ((0, 0), (0, 3), (0, 336))),
        ],
        axis=1,
    )
    rows = sum_direct(rows, "x", 0)
    packed = jnp.concatenate(
        [
            rows[:36].reshape(3, 2, 6, 384).transpose(1, 0, 2, 3).reshape(2, 18, 384),
            jnp.pad(rows[36, :48].reshape(2, 1, 24), ((0, 0), (0, 5), (0, 360))),
        ],
        axis=1,
    )
    core = coord("core")
    mine = block(packed, core, 0)
    theirs = send(block(packed, 1 - core, 0), "core", 1)
    qkv_rows = lambda v: v[:18].reshape(3, 6, 384).transpose(1, 0, 2).reshape(6, 1152)
    return pair_join(qkv_rows(mine), qkv_rows(theirs), 1), mine[18, :24] + theirs[18, :24]


def gather_params(ln1_gain, ln1_bias, qkv, qkv_bias, out, out_bias, ln2_gain, ln2_bias, fc1, fc1_bias, fc2, fc2_bias):
    small = jnp.concatenate(
        [ln1_gain, ln1_bias, qkv_bias, out_bias, ln2_gain, ln2_bias, fc1_bias, fc2_bias]
    )
    packed = jnp.concatenate(
        [
            qkv.reshape(6, 3, 768).transpose(1, 0, 2).reshape(18, 768),
            out,
            fc1.reshape(6, 4, 768).transpose(1, 0, 2).reshape(24, 768),
            fc2,
            jnp.pad(small.reshape(1, 72), ((0, 7), (0, 696))),
        ],
        axis=0,
    )
    full = lax.all_gather(packed, "fsdp", axis=0, tiled=True).reshape(128, 80, 768)
    wide = lambda at, n: jnp.concatenate(
        [full[:, at + 6 * j : at + 6 * j + 6].reshape(768, 768) for j in range(n)], axis=1
    )
    vec = lambda at, n: full[:, 72, at : at + n].reshape(128 * n)
    return (
        vec(0, 6), vec(6, 6), wide(0, 3), vec(12, 12), wide(18, 1), vec(24, 6),
        vec(30, 6), vec(36, 6), wide(24, 4), vec(42, 24), full[:, 48:72].reshape(3072, 768), vec(66, 6),
    )


def local(
    images,
    counts,
    ln1_gain,
    ln1_bias,
    qkv_weight,
    qkv_bias,
    out_weight,
    out_bias,
    ln2_gain,
    ln2_bias,
    fc1_weight,
    fc1_bias,
    fc2_weight,
    fc2_bias,
    d_out,
):
    slot_count, seq_len, feature_width = images.shape
    row_count = slot_count * seq_len
    score_scale = 1.0 / math.sqrt(HD)
    full = gather_params(
        ln1_gain, ln1_bias, qkv_weight, qkv_bias, out_weight, out_bias,
        ln2_gain, ln2_bias, fc1_weight, fc1_bias, fc2_weight, fc2_bias,
    )
    attn_full, mlp_full = full[:6], full[6:]
    gain_one, offset_one, qkv_matrix, qkv_offset, out_matrix, out_offset = attn_full
    gain_one = gain_one.astype(jnp.float32)
    offset_one = offset_one.astype(jnp.float32)
    slot_live = (jnp.arange(slot_count, dtype=jnp.int32) < counts[0]).astype(jnp.float32)
    row_live = jnp.repeat(slot_live, seq_len)[:, None]
    inputs = images.reshape(row_count, feature_width).astype(jnp.float32)
    normed_one = normalize(inputs, gain_one, offset_one).astype(jnp.bfloat16)
    bias_full = jnp.concatenate(
        [
            qkv_offset[:feature_width].astype(jnp.float32),
            jnp.zeros((feature_width,), jnp.float32),
            qkv_offset[feature_width:].astype(jnp.float32),
        ]
    )
    project = (mat_product(normed_one, qkv_matrix) + bias_full).astype(jnp.bfloat16)
    queries = project[:, :feature_width].reshape(slot_count, seq_len, H, HD)
    key_heads = project[:, feature_width : 2 * feature_width].reshape(slot_count, seq_len, H, HD)
    value_heads = project[:, 2 * feature_width :].reshape(slot_count, seq_len, H, HD)
    scores = (
        jnp.einsum("gqhd,gkhd->ghqk", queries, key_heads, preferred_element_type=jnp.float32)
        * score_scale
    )
    log_total = jax.nn.logsumexp(scores, axis=-1, keepdims=True)
    probs_low = jnp.exp(scores - log_total).astype(jnp.bfloat16)
    mixed_heads = jnp.einsum(
        "ghqk,gkhd->gqhd", probs_low, value_heads, preferred_element_type=jnp.float32
    )
    mixed_low = mixed_heads.reshape(row_count, feature_width).astype(jnp.bfloat16)
    after_attn = inputs + mat_product(mixed_low, out_matrix) + out_offset.astype(jnp.float32)
    gain_two = mlp_full[0].astype(jnp.float32)
    offset_two = mlp_full[1].astype(jnp.float32)
    normed_two = normalize(after_attn, gain_two, offset_two).astype(jnp.bfloat16)
    pre_act = mat_product(normed_two, mlp_full[2]) + mlp_full[3].astype(jnp.float32)
    hidden, gelu_back = jax.vjp(exact_gelu, pre_act)
    hidden_low = hidden.astype(jnp.bfloat16)
    branch_two = mat_product(hidden_low, mlp_full[4]) + mlp_full[5].astype(jnp.float32)
    out_images = (
        ((after_attn + branch_two) * row_live)
        .reshape(slot_count, seq_len, feature_width)
        .astype(jnp.bfloat16)
    )
    mlp_back = mlp_full
    g_branch_f = d_out.reshape(row_count, feature_width).astype(jnp.float32) * row_live
    g_branch = g_branch_f.astype(jnp.bfloat16)
    d_fc2_bias = column_sums(g_branch)
    fc2_half = pair_grad(hidden_low, g_branch)
    g_hidden = grad_input(g_branch, mlp_back[4])
    g_pre = gelu_back(g_hidden)[0].astype(jnp.bfloat16)
    d_fc1_bias = column_sums(g_pre)
    fc1_half = pair_grad(normed_two, g_pre)
    g_normed_two = grad_input(g_pre, mlp_back[2])
    norm_two_back = jax.vjp(normalize, after_attn, gain_two, offset_two)[1]
    g_after_part, d_ln2_gain, d_ln2_bias = norm_two_back(g_normed_two)
    g_after = g_branch_f + g_after_part
    attn_back = attn_full
    g_attn = g_after.astype(jnp.bfloat16)
    d_out_bias = column_sums(g_attn)
    out_half = pair_grad(mixed_low, g_attn)
    g_mixed = (
        grad_input(g_attn, attn_back[4]).astype(jnp.bfloat16).reshape(slot_count, seq_len, H, HD)
    )
    scores_again = (
        jnp.einsum("gqhd,gkhd->ghqk", queries, key_heads, preferred_element_type=jnp.float32)
        * score_scale
    )
    probs_again = jnp.exp(scores_again - log_total)
    g_probs = jnp.einsum(
        "gqhd,gkhd->ghqk", g_mixed, value_heads, preferred_element_type=jnp.float32
    )
    g_values = jnp.einsum(
        "ghqk,gqhd->gkhd",
        probs_again.astype(jnp.bfloat16),
        g_mixed,
        preferred_element_type=jnp.float32,
    )
    row_delta = jnp.sum(g_probs * probs_again, axis=-1, keepdims=True)
    g_scores = (probs_again * (g_probs - row_delta)).astype(jnp.bfloat16)
    g_queries = (
        jnp.einsum("ghqk,gkhd->gqhd", g_scores, key_heads, preferred_element_type=jnp.float32)
        * score_scale
    )
    g_keys = (
        jnp.einsum("ghqk,gqhd->gkhd", g_scores, queries, preferred_element_type=jnp.float32)
        * score_scale
    )
    g_qkv = jnp.concatenate(
        [
            g_queries.reshape(row_count, feature_width),
            g_keys.reshape(row_count, feature_width),
            g_values.reshape(row_count, feature_width),
        ],
        axis=1,
    ).astype(jnp.bfloat16)
    qkv_sums = column_sums(g_qkv)
    d_qkv_bias = jnp.concatenate([qkv_sums[:feature_width], qkv_sums[2 * feature_width :]])
    qkv_half = pair_grad(normed_one, g_qkv)
    g_normed_one = grad_input(g_qkv, attn_back[2])
    norm_one_back = jax.vjp(normalize, inputs, gain_one, offset_one)[1]
    g_input_part, d_ln1_gain, d_ln1_bias = norm_one_back(g_normed_one)
    d_images = (
        (g_after + g_input_part).reshape(slot_count, seq_len, feature_width).astype(jnp.bfloat16)
    )
    per = lambda v: v.reshape(128, -1)
    small_early = jnp.concatenate(
        [per(d_out_bias), per(d_ln2_gain), per(d_ln2_bias), per(d_fc1_bias), per(d_fc2_bias)], 1
    )
    small_late = jnp.concatenate([per(d_ln1_gain), per(d_ln1_bias), per(d_qkv_bias)], 1)
    d_fc2, d_fc1, d_out_w, early = early_sums(fc2_half, fc1_half, out_half, small_early)
    d_qkv, late = late_sums(qkv_half, small_late)
    return (
        out_images, d_images, late[:6], late[6:12], d_qkv, late[12:24], d_out_w, early[:6],
        early[6:12], early[12:18], d_fc1, early[18:42], d_fc2, early[42:48],
    )


def solution(mesh):
    in_specs = (
        P("fsdp", None, None),
        P("fsdp"),
        P("fsdp"),
        P("fsdp"),
        P("fsdp", None),
        P("fsdp"),
        P("fsdp", None),
        P("fsdp"),
        P("fsdp"),
        P("fsdp"),
        P("fsdp", None),
        P("fsdp"),
        P("fsdp", None),
        P("fsdp"),
        P("fsdp", None, None),
    )
    out_specs = (
        P("fsdp", None, None),
        P("fsdp", None, None),
        P("fsdp"),
        P("fsdp"),
        P("fsdp", None),
        P("fsdp"),
        P("fsdp", None),
        P("fsdp"),
        P("fsdp"),
        P("fsdp"),
        P("fsdp", None),
        P("fsdp"),
        P("fsdp", None),
        P("fsdp"),
    )
    return jax.shard_map(local, mesh=mesh, in_specs=in_specs, out_specs=out_specs, check_vma=False)
```

```python
import math

import jax
import jax.numpy as jnp
import numpy as np
from jax import lax
from jax.sharding import PartitionSpec as P

H = 12
HD = 64
ROWS = 208


eps_norm = 1e-06


def normalize(values, gain_vec, offset):
    average = jnp.mean(values, -1, keepdims=True)
    centered = values - average
    spread = jnp.mean(centered * centered, -1, keepdims=True)
    return centered * lax.rsqrt(spread + eps_norm) * gain_vec + offset


def gelu_parts(values):
    bell = jnp.exp(-0.5 * values * values)
    step = 1.0 / (1.0 + (0.3275911 / math.sqrt(2.0)) * jnp.abs(values))
    series = 1.061405429
    for term in (-1.453152027, 1.421413741, -0.284496736, 0.254829592):
        series = series * step + term
    tail = 0.5 * series * step * bell
    share = jnp.where(values >= 0, 1.0 - tail, tail)
    return values * share, share + values * bell * (1.0 / math.sqrt(2.0 * math.pi))


def mat_product(left, right):
    return jnp.dot(left, right, preferred_element_type=jnp.float32)


def grad_weight(left, right):
    return jnp.einsum("ra,rb->ab", left, right, preferred_element_type=jnp.float32)


def grad_input(grad_low, matrix):
    return jnp.einsum("rb,ab->ra", grad_low, matrix, preferred_element_type=jnp.float32)


def column_sums(grad_low):
    return jnp.sum(grad_low, axis=0, dtype=jnp.float32)


def torus_perm(axis, offset):
    grid = np.arange(128).reshape(4, 4, 4, 2)
    dim = {"z": 0, "y": 1, "x": 2, "core": 3}[axis]
    return list(zip(grid.reshape(-1).tolist(), np.roll(grid, -offset, dim).reshape(-1).tolist()))


def coord(axis):
    stride, size = {"z": (32, 4), "y": (8, 4), "x": (2, 4), "core": (1, 2)}[axis]
    return lax.rem(lax.div(lax.axis_index("fsdp"), jnp.int32(stride)), jnp.int32(size))


PLANE_GROUPS = np.arange(128).reshape(16, 8).T.tolist()


def send(values, axis, offset):
    return lax.ppermute(values, "fsdp", torus_perm(axis, offset))


def up(values):
    return values.astype(jnp.float32)


def down(values):
    return values.astype(jnp.bfloat16)


def block(values, index, dim):
    return lax.dynamic_index_in_dim(values, index, dim, keepdims=False)


def chunks(values, axis, dim):
    own = coord(axis)
    return [block(values, lax.rem(own + k, jnp.int32(4)), dim) for k in range(4)]


def sum_ring(values, axis, dim):
    own, one, two, three = chunks(values, axis, dim)
    half = own.shape[-1] // 2
    lo = lambda v: v[..., :half]
    hi = lambda v: v[..., half:]
    fore = send(jnp.concatenate([lo(two), hi(one)], -1), axis, 1)
    back = send(jnp.concatenate([hi(two), lo(three)], -1), axis, -1)
    fore_end = send(down(up(lo(one)) + up(lo(fore))), axis, 1)
    back_end = send(down(up(hi(three)) + up(lo(back))), axis, -1)
    low = up(lo(own)) + up(hi(back)) + up(fore_end)
    high = up(hi(own)) + up(hi(fore)) + up(back_end)
    return down(jnp.concatenate([low, high], -1))


def sum_direct(values, axis, dim):
    own, one, two, three = chunks(values, axis, dim)
    return up(own) + up(send(one, axis, 1)) + up(send(two, axis, 2)) + up(send(three, axis, -1))


def pair_grad(left, right, parts=1):
    core = coord("core")
    width = right.shape[1] // 2
    other = lax.dynamic_slice_in_dim(right, (1 - core) * width, width, 1)
    mine = lax.dynamic_slice_in_dim(right, core * width, width, 1)
    arrived = send(down(grad_weight(left, other)), "core", 1)
    step = width // parts
    return [
        down(grad_weight(left, mine[:, at : at + step]) + up(arrived[:, at : at + step]))
        for at in range(0, width, step)
    ]


def pair_join(mine, theirs, axis):
    first = coord("core") == 0
    return jnp.concatenate([jnp.where(first, mine, theirs), jnp.where(first, theirs, mine)], axis)


def pack_early(fc2, fc1, small):
    return jnp.concatenate(
        [fc2.reshape(16, 192, 384)]
        + [part.reshape(16, 48, 384) for part in fc1]
        + [jnp.pad(down(small).reshape(16, 1, 240), ((0, 0), (0, 31), (0, 144)))],
        axis=1,
    ).reshape(16 * 416, 384)


def plane_sums(packed):
    return lax.psum_scatter(
        packed, "fsdp", scatter_dimension=0, axis_index_groups=PLANE_GROUPS, tiled=True
    )


def late_sums(qkv, out, small):
    packed = jnp.concatenate([qkv.reshape(16, 48, 1152), out.reshape(16, 48, 384)], axis=2)
    small = jnp.pad(down(small).reshape(16, 1, 336), ((0, 0), (0, 15), (0, 1200)))
    packed = jnp.concatenate([packed, small], axis=1).reshape(4, 4, 64, 1536)
    first = down(sum_direct(sum_ring(packed[..., :768], "z", 0), "y", 0))
    second = down(sum_direct(sum_ring(packed[..., 768:], "y", 1), "z", 0))
    return jnp.concatenate([first, second], 1)


def last_sums(early, late):
    early, late = up(early), up(late)
    late_rows = jnp.concatenate(
        [
            late[:48].reshape(4, 12, 1536),
            jnp.pad(late[48, :336].reshape(4, 1, 84), ((0, 0), (0, 3), (0, 1452))),
        ],
        axis=1,
    )
    rows = jnp.concatenate(
        [
            early[:192].reshape(4, 48, 384),
            early[192:384].reshape(4, 4, 12, 384).transpose(1, 0, 2, 3).reshape(4, 48, 384),
        ]
        + [late_rows[:, :, 384 * j : 384 * j + 384] for j in range(4)]
        + [jnp.pad(early[384, :240].reshape(4, 1, 60), ((0, 0), (0, 7), (0, 324)))],
        axis=1,
    )
    rows = sum_direct(rows, "x", 0)
    late_part = rows[96:160].reshape(4, 16, 384)
    small = jnp.concatenate([rows[160, :60].reshape(2, 30), late_part[0, 12, :84].reshape(2, 42)], 1)
    packed = jnp.concatenate(
        [
            rows[:48].reshape(2, 24, 384),
            rows[48:96].reshape(4, 2, 6, 384).transpose(1, 0, 2, 3).reshape(2, 24, 384),
            late_part[:, :12].reshape(4, 2, 6, 384).transpose(1, 0, 2, 3).reshape(2, 24, 384),
            jnp.pad(small.reshape(2, 1, 72), ((0, 0), (0, 7), (0, 312))),
        ],
        axis=1,
    )
    core = coord("core")
    mine = block(packed, core, 0)
    theirs = send(block(packed, 1 - core, 0), "core", 1)
    wide = lambda v: v.reshape(4, 6, 384).transpose(1, 0, 2).reshape(6, 1536)
    fc2 = pair_join(mine[:24], theirs[:24], 1)
    fc1 = pair_join(wide(mine[24:48]), wide(theirs[24:48]), 1)
    late_mine, late_theirs = wide(mine[48:72]), wide(theirs[48:72])
    qkv = pair_join(late_mine[:, :1152], late_theirs[:, :1152], 1)
    out = pair_join(late_mine[:, 1152:], late_theirs[:, 1152:], 1)
    return fc2, fc1, qkv, out, mine[72, :72] + theirs[72, :72]


def gather_params(ln1_gain, ln1_bias, qkv, qkv_bias, out, out_bias, ln2_gain, ln2_bias, fc1, fc1_bias, fc2, fc2_bias):
    small = jnp.concatenate(
        [ln1_gain, ln1_bias, qkv_bias, out_bias, ln2_gain, ln2_bias, fc1_bias, fc2_bias]
    )
    wide = jnp.concatenate([qkv, out, fc1], axis=1)
    wide = jnp.concatenate([wide, jnp.pad(small.reshape(1, 72), ((0, 1), (0, 6144 - 72)))], axis=0)
    packed = jnp.concatenate([wide, fc2.reshape(3, 8, 768).transpose(1, 0, 2).reshape(8, 2304)], 1)
    full = lax.all_gather(packed[None], "fsdp", axis=0, tiled=True).reshape(1024, 8448)
    row = lax.broadcasted_iota(jnp.int32, (768, 1024), 0)
    slot = lax.broadcasted_iota(jnp.int32, (768, 1024), 1)
    pick = lax.optimization_barrier((slot == row // 6 * 8 + row % 6).astype(jnp.bfloat16))
    matrix = lambda at, n: down(mat_product(pick, full[:, at : at + n]))
    rows = full.reshape(128, 8, 8448)[:, 6, :72]
    vec = lambda at, n: rows[:, at : at + n].reshape(128 * n)
    fc2_full = full[:, 6144:].reshape(128, 8, 3, 768).transpose(0, 2, 1, 3).reshape(3072, 768)
    return (
        vec(0, 6), vec(6, 6), matrix(0, 2304), vec(12, 12), matrix(2304, 768), vec(24, 6),
        vec(30, 6), vec(36, 6), matrix(3072, 3072), vec(42, 24), fc2_full, vec(66, 6),
    )


def pairs(values):
    return jnp.stack([values[:, :, at : at + 128] for at in range(0, 768, 128)], axis=1)


def unpairs(values):
    return jnp.concatenate([values[:, at] for at in range(6)], axis=-1)


def by_head(values):
    first = jnp.arange(128) < HD
    zero = jnp.zeros_like(values)
    return jnp.concatenate(
        [jnp.where(first, values, zero), jnp.where(first, zero, values)], axis=2
    )


def own_lanes(values):
    first = jnp.arange(128) < HD
    return jnp.where(first, values[:, :, :ROWS], values[:, :, ROWS:])


def batched(form, left, right):
    return jnp.einsum(form, left, right, preferred_element_type=jnp.float32)


def attention(qkv, seq_len):
    q, k, v = (pairs(qkv[:, :, 768 * i : 768 * i + 768]) for i in range(3))
    q = by_head(q)
    scores = batched("gprd,gpkd->gprk", q, k) * (1.0 / math.sqrt(HD))
    scores = jnp.where(jnp.arange(ROWS) < seq_len, scores, -1e30)
    weight = jnp.exp(scores - jnp.max(scores, axis=-1, keepdims=True))
    probs = down(weight * (1.0 / jnp.sum(weight, axis=-1, keepdims=True)))
    mixed = unpairs(down(own_lanes(batched("gprk,gpkd->gprd", probs, v))))
    return mixed, (q, k, v, probs)


def attention_back(kept, g_mixed):
    q, k, v, probs_low = kept
    scale = 1.0 / math.sqrt(HD)
    g_mixed = by_head(pairs(g_mixed))
    probs = up(probs_low)
    g_probs = batched("gprd,gpkd->gprk", g_mixed, v)
    delta = jnp.sum(g_probs * probs, axis=-1, keepdims=True)
    g_scores = down(probs * (g_probs - delta))
    g_q = down(own_lanes(batched("gprk,gpkd->gprd", g_scores, k)) * scale)
    g_k = down(batched("gprk,gprd->gpkd", g_scores, q) * scale)
    g_v = down(batched("gprk,gprd->gpkd", probs_low, g_mixed))
    return jnp.concatenate([unpairs(g_q), unpairs(g_k), unpairs(g_v)], axis=-1)


def local(
    images,
    counts,
    ln1_gain,
    ln1_bias,
    qkv_weight,
    qkv_bias,
    out_weight,
    out_bias,
    ln2_gain,
    ln2_bias,
    fc1_weight,
    fc1_bias,
    fc2_weight,
    fc2_bias,
    d_out,
):
    slot_count, seq_len, feature_width = images.shape
    row_count = slot_count * ROWS
    pad_rows = lambda v: jnp.pad(v, ((0, 0), (0, ROWS - seq_len), (0, 0)))
    full = gather_params(
        ln1_gain, ln1_bias, qkv_weight, qkv_bias, out_weight, out_bias,
        ln2_gain, ln2_bias, fc1_weight, fc1_bias, fc2_weight, fc2_bias,
    )
    attn_full, mlp_full = full[:6], full[6:]
    gain_one, offset_one, qkv_matrix, qkv_offset, out_matrix, out_offset = attn_full
    gain_one = gain_one.astype(jnp.float32)
    offset_one = offset_one.astype(jnp.float32)
    slot_live = (jnp.arange(slot_count, dtype=jnp.int32) < counts[0]).astype(jnp.float32)
    row_live = jnp.repeat(slot_live, ROWS)[:, None]
    inputs = pad_rows(images).reshape(row_count, feature_width).astype(jnp.float32)
    normed_one = normalize(inputs, gain_one, offset_one).astype(jnp.bfloat16)
    bias_full = jnp.concatenate(
        [
            qkv_offset[:feature_width].astype(jnp.float32),
            jnp.zeros((feature_width,), jnp.float32),
            qkv_offset[feature_width:].astype(jnp.float32),
        ]
    )
    project = (mat_product(normed_one, qkv_matrix) + bias_full).astype(jnp.bfloat16)
    qkv = project.reshape(slot_count, ROWS, 3 * feature_width)
    mixed, kept = attention(qkv, seq_len)
    mixed_low = mixed.reshape(row_count, feature_width)
    after_attn = inputs + mat_product(mixed_low, out_matrix) + out_offset.astype(jnp.float32)
    gain_two = mlp_full[0].astype(jnp.float32)
    offset_two = mlp_full[1].astype(jnp.float32)
    normed_two = normalize(after_attn, gain_two, offset_two).astype(jnp.bfloat16)
    pre_act = mat_product(normed_two, mlp_full[2]) + mlp_full[3].astype(jnp.float32)
    hidden, slope = gelu_parts(pre_act)
    hidden_low = hidden.astype(jnp.bfloat16)
    slope = slope.astype(jnp.bfloat16)
    branch_two = mat_product(hidden_low, mlp_full[4]) + mlp_full[5].astype(jnp.float32)
    out_images = (
        ((after_attn + branch_two) * row_live)
        .astype(jnp.bfloat16)
        .reshape(slot_count, ROWS, feature_width)[:, :seq_len]
    )
    mlp_back = mlp_full
    g_branch_f = pad_rows(d_out).reshape(row_count, feature_width).astype(jnp.float32) * row_live
    g_branch = g_branch_f.astype(jnp.bfloat16)
    d_fc2_bias = column_sums(g_branch)
    (fc2_half,) = pair_grad(hidden_low, g_branch)
    g_hidden = grad_input(g_branch, mlp_back[4])
    g_pre = (g_hidden * slope.astype(jnp.float32)).astype(jnp.bfloat16)
    d_fc1_bias = column_sums(g_pre)
    fc1_half = pair_grad(normed_two, g_pre, 4)
    per = lambda v: v.reshape(128, -1)
    small_early = jnp.concatenate([per(d_fc1_bias), per(d_fc2_bias)], 1)
    packed = pack_early(fc2_half, fc1_half, small_early)
    packed, g_pre = lax.optimization_barrier((packed, g_pre))
    early = plane_sums(packed)
    g_normed_two = grad_input(g_pre, mlp_back[2])
    norm_two_back = jax.vjp(normalize, after_attn, gain_two, offset_two)[1]
    g_after_part, d_ln2_gain, d_ln2_bias = norm_two_back(g_normed_two)
    g_after = g_branch_f + g_after_part
    attn_back = attn_full
    g_attn = g_after.astype(jnp.bfloat16)
    d_out_bias = column_sums(g_attn)
    (out_half,) = pair_grad(mixed_low, g_attn)
    g_mixed = grad_input(g_attn, attn_back[4]).astype(jnp.bfloat16)
    g_qkv = attention_back(kept, g_mixed.reshape(slot_count, ROWS, feature_width))
    g_qkv = g_qkv.reshape(row_count, 3 * feature_width)
    qkv_sums = column_sums(g_qkv)
    d_qkv_bias = jnp.concatenate([qkv_sums[:feature_width], qkv_sums[2 * feature_width :]])
    (qkv_half,) = pair_grad(normed_one, g_qkv)
    g_normed_one = grad_input(g_qkv, attn_back[2])
    norm_one_back = jax.vjp(normalize, inputs, gain_one, offset_one)[1]
    g_input_part, d_ln1_gain, d_ln1_bias = norm_one_back(g_normed_one)
    d_images = (
        (g_after + g_input_part)
        .astype(jnp.bfloat16)
        .reshape(slot_count, ROWS, feature_width)[:, :seq_len]
    )
    small_late = jnp.concatenate(
        [
            per(v)
            for v in (d_ln1_gain, d_ln1_bias, d_qkv_bias, d_out_bias, d_ln2_gain, d_ln2_bias)
        ],
        1,
    )
    late = late_sums(qkv_half, out_half, small_late)
    d_fc2, d_fc1, d_qkv, d_out_w, small = last_sums(early, late)
    return (
        out_images, d_images, small[30:36], small[36:42], d_qkv, small[42:54], d_out_w, small[54:60],
        small[60:66], small[66:72], d_fc1, small[:24], d_fc2, small[24:30],
    )


def solution(mesh):
    in_specs = (
        P("fsdp", None, None),
        P("fsdp"),
        P("fsdp"),
        P("fsdp"),
        P("fsdp", None),
        P("fsdp"),
        P("fsdp", None),
        P("fsdp"),
        P("fsdp"),
        P("fsdp"),
        P("fsdp", None),
        P("fsdp"),
        P("fsdp", None),
        P("fsdp"),
        P("fsdp", None, None),
    )
    out_specs = (
        P("fsdp", None, None),
        P("fsdp", None, None),
        P("fsdp"),
        P("fsdp"),
        P("fsdp", None),
        P("fsdp"),
        P("fsdp", None),
        P("fsdp"),
        P("fsdp"),
        P("fsdp"),
        P("fsdp", None),
        P("fsdp"),
        P("fsdp", None),
        P("fsdp"),
    )
    return jax.shard_map(local, mesh=mesh, in_specs=in_specs, out_specs=out_specs, check_vma=False)
```

```python
import math

import jax
import jax.numpy as jnp
import numpy as np
from jax import lax
from jax.sharding import PartitionSpec as P

H = 12
HD = 64
ROWS = 208


eps_norm = 1e-06


def normalize(values, gain_vec, offset):
    average = jnp.mean(values, -1, keepdims=True)
    centered = values - average
    spread = jnp.mean(centered * centered, -1, keepdims=True)
    return centered * lax.rsqrt(spread + eps_norm) * gain_vec + offset


def gelu_parts(values):
    bell = jnp.exp(-0.5 * values * values)
    step = 1.0 / (1.0 + (0.3275911 / math.sqrt(2.0)) * jnp.abs(values))
    series = 1.061405429
    for term in (-1.453152027, 1.421413741, -0.284496736, 0.254829592):
        series = series * step + term
    tail = 0.5 * series * step * bell
    share = jnp.where(values >= 0, 1.0 - tail, tail)
    return values * share, share + values * bell * (1.0 / math.sqrt(2.0 * math.pi))


def mat_product(left, right):
    return jnp.dot(left, right, preferred_element_type=jnp.float32)


def grad_weight(left, right):
    return jnp.einsum("ra,rb->ab", left, right, preferred_element_type=jnp.float32)


def grad_input(grad_low, matrix):
    return jnp.einsum("rb,ab->ra", grad_low, matrix, preferred_element_type=jnp.float32)


def column_sums(grad_low):
    return jnp.sum(grad_low, axis=0, dtype=jnp.float32)


def torus_perm(axis, offset):
    grid = np.arange(128).reshape(4, 4, 4, 2)
    dim = {"z": 0, "y": 1, "x": 2, "core": 3}[axis]
    return list(zip(grid.reshape(-1).tolist(), np.roll(grid, -offset, dim).reshape(-1).tolist()))


def coord(axis):
    stride, size = {"z": (32, 4), "y": (8, 4), "x": (2, 4), "core": (1, 2)}[axis]
    return lax.rem(lax.div(lax.axis_index("fsdp"), jnp.int32(stride)), jnp.int32(size))


PLANE_GROUPS = np.arange(128).reshape(16, 8).T.tolist()


def send(values, axis, offset):
    return lax.ppermute(values, "fsdp", torus_perm(axis, offset))


def up(values):
    return values.astype(jnp.float32)


def down(values):
    return values.astype(jnp.bfloat16)


def block(values, index, dim):
    return lax.dynamic_index_in_dim(values, index, dim, keepdims=False)


def chunks(values, axis, dim):
    own = coord(axis)
    return [block(values, lax.rem(own + k, jnp.int32(4)), dim) for k in range(4)]


def sum_ring(values, axis, dim):
    own, one, two, three = chunks(values, axis, dim)
    half = own.shape[-1] // 2
    lo = lambda v: v[..., :half]
    hi = lambda v: v[..., half:]
    fore = send(jnp.concatenate([lo(two), hi(one)], -1), axis, 1)
    back = send(jnp.concatenate([hi(two), lo(three)], -1), axis, -1)
    fore_end = send(down(up(lo(one)) + up(lo(fore))), axis, 1)
    back_end = send(down(up(hi(three)) + up(lo(back))), axis, -1)
    low = up(lo(own)) + up(hi(back)) + up(fore_end)
    high = up(hi(own)) + up(hi(fore)) + up(back_end)
    return down(jnp.concatenate([low, high], -1))


def sum_direct(values, axis, dim):
    own, one, two, three = chunks(values, axis, dim)
    return up(own) + up(send(one, axis, 1)) + up(send(two, axis, 2)) + up(send(three, axis, -1))


def pair_grad(left, right, parts=1):
    core = coord("core")
    width = right.shape[1] // 2
    other = lax.dynamic_slice_in_dim(right, (1 - core) * width, width, 1)
    mine = lax.dynamic_slice_in_dim(right, core * width, width, 1)
    arrived = send(down(grad_weight(left, other)), "core", 1)
    step = width // parts
    return [
        down(grad_weight(left, mine[:, at : at + step]) + up(arrived[:, at : at + step]))
        for at in range(0, width, step)
    ]


def pair_join(mine, theirs, axis):
    first = coord("core") == 0
    return jnp.concatenate([jnp.where(first, mine, theirs), jnp.where(first, theirs, mine)], axis)


def pack_early(fc2, fc1, small):
    return jnp.concatenate(
        [fc2.reshape(16, 192, 384)]
        + [part.reshape(16, 48, 384) for part in fc1]
        + [jnp.pad(down(small).reshape(16, 1, 240), ((0, 0), (0, 31), (0, 144)))],
        axis=1,
    ).reshape(16 * 416, 384)


def plane_sums(packed):
    return lax.psum_scatter(
        packed, "fsdp", scatter_dimension=0, axis_index_groups=PLANE_GROUPS, tiled=True
    )


def late_sums(qkv, out, small):
    packed = jnp.concatenate([qkv.reshape(16, 48, 1152), out.reshape(16, 48, 384)], axis=2)
    small = jnp.pad(down(small).reshape(16, 1, 336), ((0, 0), (0, 15), (0, 1200)))
    packed = jnp.concatenate([packed, small], axis=1).reshape(4, 4, 64, 1536)
    first = down(sum_direct(sum_ring(packed[..., :768], "z", 0), "y", 0))
    second = down(sum_direct(sum_ring(packed[..., 768:], "y", 1), "z", 0))
    return jnp.concatenate([first, second], 1)


def last_sums(early, late):
    early, late = up(early), up(late)
    late_rows = jnp.concatenate(
        [
            late[:48].reshape(4, 12, 1536),
            jnp.pad(late[48, :336].reshape(4, 1, 84), ((0, 0), (0, 3), (0, 1452))),
        ],
        axis=1,
    )
    rows = jnp.concatenate(
        [
            early[:192].reshape(4, 48, 384),
            early[192:384].reshape(4, 4, 12, 384).transpose(1, 0, 2, 3).reshape(4, 48, 384),
        ]
        + [late_rows[:, :, 384 * j : 384 * j + 384] for j in range(4)]
        + [jnp.pad(early[384, :240].reshape(4, 1, 60), ((0, 0), (0, 7), (0, 324)))],
        axis=1,
    )
    rows = sum_direct(rows, "x", 0)
    late_part = rows[96:160].reshape(4, 16, 384)
    small = jnp.concatenate([rows[160, :60].reshape(2, 30), late_part[0, 12, :84].reshape(2, 42)], 1)
    packed = jnp.concatenate(
        [
            rows[:48].reshape(2, 24, 384),
            rows[48:96].reshape(4, 2, 6, 384).transpose(1, 0, 2, 3).reshape(2, 24, 384),
            late_part[:, :12].reshape(4, 2, 6, 384).transpose(1, 0, 2, 3).reshape(2, 24, 384),
            jnp.pad(small.reshape(2, 1, 72), ((0, 0), (0, 7), (0, 312))),
        ],
        axis=1,
    )
    core = coord("core")
    mine = block(packed, core, 0)
    theirs = send(block(packed, 1 - core, 0), "core", 1)
    wide = lambda v: v.reshape(4, 6, 384).transpose(1, 0, 2).reshape(6, 1536)
    fc2 = pair_join(mine[:24], theirs[:24], 1)
    fc1 = pair_join(wide(mine[24:48]), wide(theirs[24:48]), 1)
    late_mine, late_theirs = wide(mine[48:72]), wide(theirs[48:72])
    qkv = pair_join(late_mine[:, :1152], late_theirs[:, :1152], 1)
    out = pair_join(late_mine[:, 1152:], late_theirs[:, 1152:], 1)
    return fc2, fc1, qkv, out, mine[72, :72] + theirs[72, :72]


def gather_params(ln1_gain, ln1_bias, qkv, qkv_bias, out, out_bias, ln2_gain, ln2_bias, fc1, fc1_bias, fc2, fc2_bias):
    small = jnp.concatenate(
        [ln1_gain, ln1_bias, qkv_bias, out_bias, ln2_gain, ln2_bias, fc1_bias, fc2_bias]
    )
    wide = jnp.concatenate([qkv, out, fc1], axis=1)
    wide = jnp.concatenate([wide, jnp.pad(small.reshape(1, 72), ((0, 1), (0, 6144 - 72)))], axis=0)
    packed = jnp.concatenate([wide, fc2.reshape(3, 8, 768).transpose(1, 0, 2).reshape(8, 2304)], 1)
    full = lax.all_gather(packed[None], "fsdp", axis=0, tiled=True).reshape(1024, 8448)
    row = lax.broadcasted_iota(jnp.int32, (768, 1024), 0)
    slot = lax.broadcasted_iota(jnp.int32, (768, 1024), 1)
    pick = lax.optimization_barrier((slot == row // 6 * 8 + row % 6).astype(jnp.bfloat16))
    matrix = lambda at, n: down(mat_product(pick, full[:, at : at + n]))
    rows = full.reshape(128, 8, 8448)[:, 6, :72]
    vec = lambda at, n: rows[:, at : at + n].reshape(128 * n)
    fc2_full = full[:, 6144:].reshape(128, 8, 3, 768).transpose(0, 2, 1, 3).reshape(3072, 768)
    return (
        vec(0, 6), vec(6, 6), matrix(0, 2304), vec(12, 12), matrix(2304, 768), vec(24, 6),
        vec(30, 6), vec(36, 6), matrix(3072, 3072), vec(42, 24), fc2_full, vec(66, 6),
    )


def pairs(values):
    return values.reshape(values.shape[0], ROWS, -1, 128).transpose(0, 2, 1, 3)


def unpairs(values):
    return values.transpose(0, 2, 1, 3).reshape(values.shape[0], ROWS, -1)


def by_head(values):
    first = jnp.arange(128) < HD
    zero = jnp.zeros_like(values)
    return jnp.concatenate(
        [jnp.where(first, values, zero), jnp.where(first, zero, values)], axis=2
    )


def own_lanes(values):
    first = jnp.arange(128) < HD
    return jnp.where(first, values[:, :, :ROWS], values[:, :, ROWS:])


def batched(form, left, right):
    return jnp.einsum(form, left, right, preferred_element_type=jnp.float32)


def attention(qkv, seq_len):
    blocks = pairs(qkv)
    q, k, v = by_head(blocks[:, :6]), blocks[:, 6:12], blocks[:, 12:]
    scores = batched("gprd,gpkd->gprk", q, k) * (1.0 / math.sqrt(HD))
    scores = jnp.where(jnp.arange(ROWS) < seq_len, scores, -1e30)
    weight = jnp.exp(scores - jnp.max(scores, axis=-1, keepdims=True))
    probs = down(weight * (1.0 / jnp.sum(weight, axis=-1, keepdims=True)))
    mixed = unpairs(down(own_lanes(batched("gprk,gpkd->gprd", probs, v))))
    return mixed, (q, k, v, probs)


def attention_back(kept, g_mixed):
    q, k, v, probs_low = kept
    scale = 1.0 / math.sqrt(HD)
    g_mixed = by_head(pairs(g_mixed))
    probs = up(probs_low)
    g_probs = batched("gprd,gpkd->gprk", g_mixed, v)
    delta = jnp.sum(g_probs * probs, axis=-1, keepdims=True)
    g_scores = down(probs * (g_probs - delta))
    g_q = down(own_lanes(batched("gprk,gpkd->gprd", g_scores, k)) * scale)
    g_k = down(batched("gprk,gprd->gpkd", g_scores, q) * scale)
    g_v = down(batched("gprk,gprd->gpkd", probs_low, g_mixed))
    return unpairs(jnp.concatenate([g_q, g_k, g_v], axis=1))


def local(
    images,
    counts,
    ln1_gain,
    ln1_bias,
    qkv_weight,
    qkv_bias,
    out_weight,
    out_bias,
    ln2_gain,
    ln2_bias,
    fc1_weight,
    fc1_bias,
    fc2_weight,
    fc2_bias,
    d_out,
):
    slot_count, seq_len, feature_width = images.shape
    row_count = slot_count * ROWS
    pad_rows = lambda v: jnp.pad(v, ((0, 0), (0, ROWS - seq_len), (0, 0)))
    full = gather_params(
        ln1_gain, ln1_bias, qkv_weight, qkv_bias, out_weight, out_bias,
        ln2_gain, ln2_bias, fc1_weight, fc1_bias, fc2_weight, fc2_bias,
    )
    attn_full, mlp_full = full[:6], full[6:]
    gain_one, offset_one, qkv_matrix, qkv_offset, out_matrix, out_offset = attn_full
    gain_one = gain_one.astype(jnp.float32)
    offset_one = offset_one.astype(jnp.float32)
    slot_live = (jnp.arange(slot_count, dtype=jnp.int32) < counts[0]).astype(jnp.float32)
    row_live = jnp.repeat(slot_live, ROWS)[:, None]
    inputs = pad_rows(images).reshape(row_count, feature_width).astype(jnp.float32)
    normed_one = normalize(inputs, gain_one, offset_one).astype(jnp.bfloat16)
    bias_full = jnp.concatenate(
        [
            qkv_offset[:feature_width].astype(jnp.float32),
            jnp.zeros((feature_width,), jnp.float32),
            qkv_offset[feature_width:].astype(jnp.float32),
        ]
    )
    project = (mat_product(normed_one, qkv_matrix) + bias_full).astype(jnp.bfloat16)
    qkv = project.reshape(slot_count, ROWS, 3 * feature_width)
    mixed, kept = attention(qkv, seq_len)
    mixed_low = mixed.reshape(row_count, feature_width)
    after_attn = inputs + mat_product(mixed_low, out_matrix) + out_offset.astype(jnp.float32)
    gain_two = mlp_full[0].astype(jnp.float32)
    offset_two = mlp_full[1].astype(jnp.float32)
    normed_two = normalize(after_attn, gain_two, offset_two).astype(jnp.bfloat16)
    pre_act = mat_product(normed_two, mlp_full[2]) + mlp_full[3].astype(jnp.float32)
    hidden, slope = gelu_parts(pre_act)
    hidden_low = hidden.astype(jnp.bfloat16)
    slope = slope.astype(jnp.bfloat16)
    branch_two = mat_product(hidden_low, mlp_full[4]) + mlp_full[5].astype(jnp.float32)
    out_images = (
        ((after_attn + branch_two) * row_live)
        .astype(jnp.bfloat16)
        .reshape(slot_count, ROWS, feature_width)[:, :seq_len]
    )
    mlp_back = mlp_full
    g_branch_f = pad_rows(d_out).reshape(row_count, feature_width).astype(jnp.float32) * row_live
    g_branch = g_branch_f.astype(jnp.bfloat16)
    d_fc2_bias = column_sums(g_branch)
    (fc2_half,) = pair_grad(hidden_low, g_branch)
    g_hidden = grad_input(g_branch, mlp_back[4])
    g_pre = (g_hidden * slope.astype(jnp.float32)).astype(jnp.bfloat16)
    d_fc1_bias = column_sums(g_pre)
    fc1_half = pair_grad(normed_two, g_pre, 4)
    per = lambda v: v.reshape(128, -1)
    small_early = jnp.concatenate([per(d_fc1_bias), per(d_fc2_bias)], 1)
    packed = pack_early(fc2_half, fc1_half, small_early)
    packed, g_pre = lax.optimization_barrier((packed, g_pre))
    early = plane_sums(packed)
    g_normed_two = grad_input(g_pre, mlp_back[2])
    norm_two_back = jax.vjp(normalize, after_attn, gain_two, offset_two)[1]
    g_after_part, d_ln2_gain, d_ln2_bias = norm_two_back(g_normed_two)
    g_after = g_branch_f + g_after_part
    attn_back = attn_full
    g_attn = g_after.astype(jnp.bfloat16)
    d_out_bias = column_sums(g_attn)
    (out_half,) = pair_grad(mixed_low, g_attn)
    g_mixed = grad_input(g_attn, attn_back[4]).astype(jnp.bfloat16)
    g_qkv = attention_back(kept, g_mixed.reshape(slot_count, ROWS, feature_width))
    g_qkv = g_qkv.reshape(row_count, 3 * feature_width)
    qkv_sums = column_sums(g_qkv)
    d_qkv_bias = jnp.concatenate([qkv_sums[:feature_width], qkv_sums[2 * feature_width :]])
    (qkv_half,) = pair_grad(normed_one, g_qkv)
    g_normed_one = grad_input(g_qkv, attn_back[2])
    norm_one_back = jax.vjp(normalize, inputs, gain_one, offset_one)[1]
    g_input_part, d_ln1_gain, d_ln1_bias = norm_one_back(g_normed_one)
    d_images = (
        (g_after + g_input_part)
        .astype(jnp.bfloat16)
        .reshape(slot_count, ROWS, feature_width)[:, :seq_len]
    )
    small_late = jnp.concatenate(
        [
            per(v)
            for v in (d_ln1_gain, d_ln1_bias, d_qkv_bias, d_out_bias, d_ln2_gain, d_ln2_bias)
        ],
        1,
    )
    late = late_sums(qkv_half, out_half, small_late)
    d_fc2, d_fc1, d_qkv, d_out_w, small = last_sums(early, late)
    return (
        out_images, d_images, small[30:36], small[36:42], d_qkv, small[42:54], d_out_w, small[54:60],
        small[60:66], small[66:72], d_fc1, small[:24], d_fc2, small[24:30],
    )


def solution(mesh):
    in_specs = (
        P("fsdp", None, None),
        P("fsdp"),
        P("fsdp"),
        P("fsdp"),
        P("fsdp", None),
        P("fsdp"),
        P("fsdp", None),
        P("fsdp"),
        P("fsdp"),
        P("fsdp"),
        P("fsdp", None),
        P("fsdp"),
        P("fsdp", None),
        P("fsdp"),
        P("fsdp", None, None),
    )
    out_specs = (
        P("fsdp", None, None),
        P("fsdp", None, None),
        P("fsdp"),
        P("fsdp"),
        P("fsdp", None),
        P("fsdp"),
        P("fsdp", None),
        P("fsdp"),
        P("fsdp"),
        P("fsdp"),
        P("fsdp", None),
        P("fsdp"),
        P("fsdp", None),
        P("fsdp"),
    )
    return jax.shard_map(local, mesh=mesh, in_specs=in_specs, out_specs=out_specs, check_vma=False)
```
